256 devices in a mesh: dp: 32 (over y, z), tensor: 4 (over x_lo, core), query: 2 (over x_hi).
Axes of the slice: x: 4 (x_hi: 2, x_lo: 2; x = x_hi * 2 + x_lo), y: 4, z: 8, core: 2. Of those that a mesh axis runs over, the one named last changes fastest.
Arguments:
- hidden_acts: bfloat16 [65536, 14336], P(('dp', 'query'), 'tensor'), may hold values from -6 to 6
- out_grads: bfloat16 [65536, 4096], P(('dp', 'query'), 'tensor'), may hold values from -6 to 6
- proj_in: bfloat16 [14336, 64], P('tensor'), may hold values from -0.046875 to 0.046875
- proj_out: bfloat16 [4096, 64], P('tensor'), may hold values from -0.09375 to 0.09375
- queries: bfloat16 [2048, 4096], P('query', 'dp'), may hold values from -1.5 to 1.5
- owner: int32 [256], P('dp'), may hold values from 0 to 31
Outputs:
- scores: float32 [256, 2048], P('dp', 'query')
- owner_totals: float32 [32, 2048], P('dp', 'query')
The draws below stay inside these ranges and needn't reach their ends.
Inputs may be any that keep to these rules, and one draw needn't show every extreme that they name: owner index of each example.
All inputs are finite; a program needn't handle non-finite values.
Results may differ from the reference program's by a relative error of at most 0.005.
Values may be sent and summed in bfloat16 or wider, within the bound.
A program may use at most 64 MiB of HBM per device.

```python
import jax
import jax.numpy as jnp
from jax import lax

D = 4096
FF = 14336
RANK = 64
TOK = 256
KK = 4096
EXAMPLES = 256
ROWS = 65536
NQ = 2048
OWNERS = 32


def place_ends(entries, stream_key, low, top_value):
    longest = entries.shape.index(max(entries.shape))
    spots = []
    for shift in (0, 1):
        where = [jax.random.randint(jax.random.fold_in(stream_key, axis), (), 0, length) for axis, length in enumerate(entries.shape)]
        where[longest] = (where[longest] + shift) % entries.shape[longest]
        spots.append(tuple(where))
    return entries.at[spots[0]].set(low).at[spots[1]].set(top_value)


def block_levels(stream_key, extent, cuts, low, largest):
    def one(position, blocks):
        steps = jax.random.uniform(jax.random.fold_in(jax.random.fold_in(stream_key, 6), position), (blocks,), jnp.float32, low / len(cuts), largest / len(cuts))
        return jnp.repeat(jnp.exp(steps), extent[position] // blocks).reshape((-1,) + (1,) * (len(extent) - position - 1))

    factor_of = one(*cuts[0])
    for cut in cuts[1:]:
        factor_of = factor_of * one(*cut)
    return factor_of


def centred(rng, shape, spread, bound, shards=(), kind=jnp.bfloat16):
    result = jax.random.normal(rng, shape, jnp.float32) * spread
    if len(shards) > 0:
        result = block_levels(rng, shape, shards, -0.22, 0.18) * result
    return jnp.clip(result, min=-bound, max=bound).astype(kind)


def setup_inputs(seed: int = 0) -> dict:
    arg_keys = jax.random.split(jax.random.key(seed), 7)
    return {
        "hidden_acts": centred(arg_keys[0], (ROWS, FF), 1.0, 6.0, ((0, 64), (1, 4))),
        "out_grads": centred(arg_keys[1], (ROWS, D), 1.0, 6.0, ((0, 64), (1, 4))),
        "proj_in": centred(arg_keys[2], (FF, RANK), FF ** -0.5, 0.046875, ((0, 4),)),
        "proj_out": centred(arg_keys[3], (D, RANK), D ** -0.5, 0.09375, ((0, 4),)),
        "queries": centred(arg_keys[4], (NQ, KK), 0.25, 1.5, ((0, 2), (1, 32))),
        "owner": place_ends(jax.random.randint(arg_keys[5], (EXAMPLES,), 0, OWNERS), jax.random.fold_in(arg_keys[5], 1), 0, OWNERS - 1).astype(jnp.int32),
    }


def example_sketch(acts_block, grads_block, proj_in, proj_out):
    left_side = jnp.dot(acts_block, proj_in, preferred_element_type=jnp.float32).astype(jnp.bfloat16)
    right_side = jnp.dot(grads_block, proj_out, preferred_element_type=jnp.float32).astype(jnp.bfloat16)
    outer = jnp.einsum("ti,tj->ij", left_side.astype(jnp.float32), right_side.astype(jnp.float32)) / TOK
    return outer.reshape(RANK * RANK).astype(jnp.bfloat16)


def reference(hidden_acts, out_grads, proj_in, proj_out, queries, owner):
    acts_all = hidden_acts.reshape(EXAMPLES, TOK, FF)
    grads_all = out_grads.reshape(EXAMPLES, TOK, D)
    sketch = lax.map(lambda pair: example_sketch(pair[0], pair[1], proj_in, proj_out), (acts_all, grads_all))
    scores = lax.dot_general(sketch, queries, (((1,), (1,)), ((), ())), preferred_element_type=jnp.float32)
    owner_onehot = (owner[:, None] == jnp.arange(OWNERS, dtype=jnp.int32)[None, :]).astype(jnp.float32)
    owner_totals = jnp.dot(owner_onehot.T, scores, precision=lax.Precision.HIGHEST)
    return scores, owner_totals
```

```python
import functools

import jax
import jax.numpy as jnp
from jax import lax
from jax.experimental import pallas as pl
from jax.experimental.pallas import tpu as pltpu
from jax.sharding import PartitionSpec as P

MESH = pl.DeviceIdType.MESH
NT = (((1,), (1,)), ((), ()))
TN = (((0,), (0,)), ((), ()))

RANK = 64
TOK = 256
NY, NZ = 4, 8
NT_DEV = 4
LINE = 8
NA, NB = 8, 4
QS = 256
CHUNK = 128
AHEAD = 3
F32, BF16 = jnp.float32, jnp.bfloat16


def dp_of(a, b):
    return b * NZ + a


def kernel(
    h_ref, g_ref, wi_ref, wo_ref, q_ref, owner_ref,
    scores_ref, totals_ref,
    hv, gv, wiv, wov, cross, mate, own, cross_in, mate_in,
    outer, sketch, land, qv, owner_s, owner_t, owner_in,
    part, opart, part_in, opart_in, sc, oo, sc_in, oo_in,
    load_sem, w_sem, misc_sem, rs_send, rs_recv, q_send, q_recv, ow_send, ow_recv,
    s1_send, s1_recv, s2_send, s2_recv, s3_send, s3_recv,
):
    dp, t, hq = lax.axis_index("dp"), lax.axis_index("tensor"), lax.axis_index("query")
    a, b = dp % NZ, dp // NZ
    m = hq * NT_DEV + t
    e_here = a * LINE + m

    far = (t + 2) % NT_DEV
    blocks = (far, far + 1 - 2 * (far % 2), t + 1 - 2 * (t % 2), t)

    def load(c):
        rows = pl.ds(pl.multiple_of(blocks[c // 2] * TOK + (c % 2) * CHUNK, CHUNK), CHUNK)
        return (
            pltpu.make_async_copy(h_ref.at[rows], hv.at[c], load_sem.at[0, c]),
            pltpu.make_async_copy(g_ref.at[rows], gv.at[c], load_sem.at[1, c]),
        )

    chunks = len(blocks) * TOK // CHUNK
    loads = [load(c) for c in range(chunks)]
    w_in = pltpu.make_async_copy(wi_ref, wiv, w_sem.at[0])
    w_out = pltpu.make_async_copy(wo_ref, wov, w_sem.at[1])
    w_in.start()
    loads[0][0].start()
    w_out.start()
    loads[0][1].start()
    for c in range(1, AHEAD):
        for copy in loads[c]:
            copy.start()
    q_rows = pl.ds(pl.multiple_of(t * QS, QS), QS)
    q_own = pltpu.make_async_copy(q_ref.at[q_rows], qv.at[b], misc_sem.at[0])
    o_own = pltpu.make_async_copy(owner_ref, owner_s, misc_sem.at[1])
    q_own.start()
    o_own.start()

    def in_plane(i):
        s = (e_here + i) % (NA * LINE)
        return {"dp": dp_of(s // LINE, b), "tensor": s % NT_DEV, "query": s % LINE // NT_DEV}, s

    def along_b(i):
        s = (b * NT_DEV + t + i) % (NB * NT_DEV)
        return {"dp": dp_of(a, s // NT_DEV), "tensor": s % NT_DEV}, s

    barrier = pltpu.get_barrier_semaphore()

    def greet_plane(i, _):
        pl.semaphore_signal(barrier, inc=1, device_id=in_plane(i)[0], device_id_type=MESH)
        return _

    def greet_b(i, _):
        to = {"dp": dp_of(a, (b + 1 + i // NT_DEV) % NB), "tensor": i % NT_DEV}
        pl.semaphore_signal(barrier, inc=1, device_id=to, device_id_type=MESH)
        return _

    lax.fori_loop(1, NA * LINE, greet_plane, 0)
    lax.fori_loop(0, (NB - 1) * NT_DEV, greet_b, 0)

    rs = []
    for c in range(chunks):
        if c + AHEAD < chunks:
            for copy in loads[c + AHEAD]:
                copy.start()
        if c == 0:
            w_in.wait()
        loads[c][0].wait()
        left = lax.dot_general(hv[c], wiv[...], NT, preferred_element_type=F32)
        if c == 0:
            w_out.wait()
        loads[c][1].wait()
        right = lax.dot_general(gv[c], wov[...], NT, preferred_element_type=F32)
        both = jnp.concatenate([left, right], axis=1)
        rows = pl.ds(c % 2 * CHUNK, CHUNK)
        if c < 4:
            cross[c // 2, rows, :] = both.astype(BF16)
        elif c < 6:
            mate[rows, :] = both
        else:
            own[rows, :] = both
        if c == 5:
            pl.semaphore_wait(barrier, NA * LINE - 1 + (NB - 1) * NT_DEV)
            for i in range(3):
                rs.append(
                    pltpu.make_async_remote_copy(
                        src_ref=cross.at[i] if i < 2 else mate,
                        dst_ref=cross_in.at[i] if i < 2 else mate_in,
                        send_sem=rs_send.at[i],
                        recv_sem=rs_recv.at[i],
                        device_id={"tensor": blocks[i]},
                        device_id_type=MESH,
                    )
                )
                rs[-1].start()

    q_own.wait()

    def send_q(i, _):
        pltpu.make_async_remote_copy(
            src_ref=q_ref.at[
                pl.ds(pl.multiple_of(t * QS, QS), QS)
            ],
            dst_ref=qv.at[b],
            send_sem=q_send,
            recv_sem=q_recv,
            device_id={"dp": dp_of(a, (b + i) % NB)},
            device_id_type=MESH,
        ).start()
        return _

    lax.fori_loop(1, NB, send_q, 0)
    o_own.wait()
    row = lax.broadcasted_iota(jnp.int32, (8, 128), 0)
    tile = jnp.zeros((8, 128), jnp.int32)
    for e in range(8):
        tile = jnp.where(row == e, owner_s[e], tile)
    owner_t[...] = tile
    owner_in[a] = tile

    def send_owner(i, _):
        pltpu.make_async_remote_copy(
            src_ref=owner_t,
            dst_ref=owner_in.at[a],
            send_sem=ow_send,
            recv_sem=ow_recv,
            device_id={"dp": dp_of((a + i) % NA, b)},
            device_id_type=MESH,
        ).start()
        return _

    lax.fori_loop(1, NA, send_owner, 0)

    for copy in rs:
        copy.wait_recv()
    whole = (
        own[...] + mate_in[...] + cross_in[0].astype(F32) + cross_in[1].astype(F32)
    ).astype(BF16)
    outer[...] = lax.dot_general(whole, whole, TN, preferred_element_type=F32) * (1.0 / TOK)
    lane = lax.broadcasted_iota(jnp.int32, (NB, 128), 1)
    for i in range(NA):
        even = outer[pl.ds(2 * i, NB, stride=2 * NZ), :]
        odd = outer[pl.ds(2 * i + 1, NB, stride=2 * NZ), :]
        sketch[i] = jnp.where(lane < RANK, pltpu.roll(even, RANK, 1), odd)
    land[e_here] = sketch[a]

    def send_sketch(i, _):
        to, s = in_plane(i)
        pltpu.make_async_remote_copy(
            src_ref=sketch.at[s // LINE],
            dst_ref=land.at[e_here],
            send_sem=s1_send,
            recv_sem=s1_recv,
            device_id=to,
            device_id_type=MESH,
        ).start()
        return _

    lax.fori_loop(1, NA * LINE, send_sketch, 0)

    def settle(ref, sem):
        pltpu.make_async_copy(ref, ref, sem).wait()

    settle(qv.at[pl.ds(0, NB - 1)], q_recv)
    settle(owner_in.at[pl.ds(0, NA - 1)], ow_recv)
    settle(land.at[pl.ds(0, NA * LINE - 1)], s1_recv)

    total = jnp.zeros((NA * LINE, QS), F32)
    for i in range(NB):
        total += lax.dot_general(
            land[:, i, :].astype(BF16), qv[i], NT, preferred_element_type=F32
        )
    part[...] = total.reshape(NA, 8, QS)
    lanes = lax.broadcasted_iota(jnp.int32, (NA * LINE, 128), 1)
    named = dp_of(lanes // NB, lanes % NB)
    onehot = (owner_in[...].reshape(NA * LINE, 128) == named).astype(F32)
    summed = lax.dot_general(
        onehot, total, TN, precision=lax.Precision.HIGHEST, preferred_element_type=F32
    )
    for i in range(NA):
        opart[i] = summed[i * NB : (i + 1) * NB]
    part_in[a] = part[a]
    opart_in[a] = opart[a]

    def send_part(i, _):
        s = (a + i) % NA
        for src, dst, k in ((part, part_in, 0), (opart, opart_in, 1)):
            pltpu.make_async_remote_copy(
                src_ref=src.at[s],
                dst_ref=dst.at[a],
                send_sem=s2_send.at[k],
                recv_sem=s2_recv.at[k],
                device_id={"dp": dp_of(s, b)},
                device_id_type=MESH,
            ).start()
        return _

    lax.fori_loop(1, NA, send_part, 0)
    settle(part_in.at[pl.ds(0, NA - 1)], s2_recv.at[0])
    settle(opart_in.at[pl.ds(0, NA - 1)], s2_recv.at[1])
    sc[...] = jnp.sum(part_in[...], axis=0)
    owned = jnp.sum(opart_in[...], axis=0)
    for i in range(NB):
        oo[i] = owned[i : i + 1]

    sc_in[t] = sc[...]
    oo_in[b * NT_DEV + t] = oo[b]

    def send_total(i, _):
        to, s = along_b(i)
        pltpu.make_async_remote_copy(
            src_ref=oo.at[s // NT_DEV],
            dst_ref=oo_in.at[b * NT_DEV + t],
            send_sem=s3_send.at[1],
            recv_sem=s3_recv.at[1],
            device_id=to,
            device_id_type=MESH,
        ).start()
        return _

    def send_scores(i, _):
        pltpu.make_async_remote_copy(
            src_ref=sc,
            dst_ref=sc_in.at[t],
            send_sem=s3_send.at[0],
            recv_sem=s3_recv.at[0],
            device_id={"tensor": (t + i) % NT_DEV},
            device_id_type=MESH,
        ).start()
        return _

    lax.fori_loop(1, NB * NT_DEV, send_total, 0)
    lax.fori_loop(1, NT_DEV, send_scores, 0)
    settle(sc_in.at[pl.ds(0, NT_DEV - 1)], s3_recv.at[0])
    for i in range(NT_DEV):
        scores_ref[:, i * QS : (i + 1) * QS] = sc_in[i]
    settle(oo_in.at[pl.ds(0, NB * NT_DEV - 1)], s3_recv.at[1])
    for i in range(NT_DEV):
        row = oo_in[i]
        for j in range(1, NB):
            row = row + oo_in[j * NT_DEV + i]
        totals_ref[:, i * QS : (i + 1) * QS] = row

    for copy in rs:
        copy.wait_send()
    settle(qv.at[pl.ds(0, NB - 1)], q_send)
    settle(owner_in.at[pl.ds(0, NA - 1)], ow_send)
    settle(land.at[pl.ds(0, NA * LINE - 1)], s1_send)
    settle(part_in.at[pl.ds(0, NA - 1)], s2_send.at[0])
    settle(opart_in.at[pl.ds(0, NA - 1)], s2_send.at[1])
    settle(sc_in.at[pl.ds(0, NT_DEV - 1)], s3_send.at[0])
    settle(oo_in.at[pl.ds(0, NB * NT_DEV - 1)], s3_send.at[1])


def shards(hidden_acts, out_grads, proj_in, proj_out, queries, owner):
    ff, d = hidden_acts.shape[1], out_grads.shape[1]
    chunks = hidden_acts.shape[0] // CHUNK
    entries = queries.shape[1]
    any_ = pl.BlockSpec(memory_space=pl.ANY)
    vmem = pl.BlockSpec(memory_space=pltpu.VMEM)
    dma = pltpu.SemaphoreType.DMA
    return pl.pallas_call(
        kernel,
        out_shape=(
            jax.ShapeDtypeStruct((8, NT_DEV * QS), F32),
            jax.ShapeDtypeStruct((1, NT_DEV * QS), F32),
        ),
        in_specs=[any_] * 6,
        out_specs=(vmem, vmem),
        scratch_shapes=[
            pltpu.VMEM((chunks, CHUNK, ff), BF16),
            pltpu.VMEM((chunks, CHUNK, d), BF16),
            pltpu.VMEM((RANK, ff), BF16),
            pltpu.VMEM((RANK, d), BF16),
            pltpu.VMEM((2, TOK, 2 * RANK), BF16),
            pltpu.VMEM((TOK, 2 * RANK), F32),
            pltpu.VMEM((TOK, 2 * RANK), F32),
            pltpu.VMEM((2, TOK, 2 * RANK), BF16),
            pltpu.VMEM((TOK, 2 * RANK), F32),
            pltpu.VMEM((128, 128), F32),
            pltpu.VMEM((NA, NB, 128), F32),
            pltpu.VMEM((NA * LINE, NB, 128), F32),
            pltpu.VMEM((NB, QS, entries), BF16),
            pltpu.SMEM((8,), jnp.int32),
            pltpu.VMEM((8, 128), jnp.int32),
            pltpu.VMEM((NA, 8, 128), jnp.int32),
            pltpu.VMEM((NA, 8, QS), F32),
            pltpu.VMEM((NA, NB, QS), F32),
            pltpu.VMEM((NA, 8, QS), F32),
            pltpu.VMEM((NA, NB, QS), F32),
            pltpu.VMEM((8, QS), F32),
            pltpu.VMEM((NB, 1, QS), F32),
            pltpu.VMEM((NT_DEV, 8, QS), F32),
            pltpu.VMEM((NB * NT_DEV, 1, QS), F32),
            dma((2, chunks)),
            dma((2,)),
            dma((2,)),
            dma((3,)),
            dma((3,)),
            dma,
            dma,
            dma,
            dma,
            dma,
            dma,
            dma((2,)),
            dma((2,)),
            dma((2,)),
            dma((2,)),
        ],
        compiler_params=pltpu.CompilerParams(
            collective_id=0, has_side_effects=True, vmem_limit_bytes=63 << 20
        ),
        name="attribution",
    )(hidden_acts, out_grads, proj_in.T, proj_out.T, queries, owner)


def solution(mesh):
    in_specs = (
        P(("dp", "query"), "tensor"),
        P(("dp", "query"), "tensor"),
        P("tensor", None),
        P("tensor", None),
        P("query", "dp"),
        P("dp"),
    )
    out_specs = (P("dp", "query"), P("dp", "query"))
    return jax.shard_map(shards, mesh=mesh, in_specs=in_specs, out_specs=out_specs, check_vma=False)
```

```python
import itertools

import jax
import jax.numpy as jnp
from jax import lax
from jax.experimental import pallas as pl
from jax.experimental.pallas import tpu as pltpu
from jax.sharding import PartitionSpec as P

MESH = pl.DeviceIdType.MESH
NT = (((1,), (1,)), ((), ()))
TN = (((0,), (0,)), ((), ()))

RANK = 64
TOK = 256
NY, NZ = 4, 8
NT_DEV = 4
LINE = 8
NA, NB = NY, NZ
NX = 4
QS = 256
CHUNK = 256
PIECES = TOK // CHUNK
AHEAD = 2
F32, BF16 = jnp.float32, jnp.bfloat16


def dp_of(a, b):
    return a * NB + b


def ring(n):
    return sorted(range(n), key=lambda i: -min(i, n - i))


def kernel(
    h_ref, g_ref, wi_ref, wo_ref, q_ref, owner_ref,
    scores_ref, totals_ref,
    hv, gv, wiv, wov, cross, mate, own, cross_in, mate_in,
    outer, sketch, land, qv, owner_s, owner_t, owner_in,
    part, opart, part_in, opart_in, sc, oo, sc_in, oo_in,
    load_sem, w_sem, misc_sem, rs_send, rs_recv, q_send, q_recv, ow_send, ow_recv,
    s1_send, s1_recv, s2_send, s2_recv, s3_send, s3_recv,
):
    dp, t, hq = lax.axis_index("dp"), lax.axis_index("tensor"), lax.axis_index("query")
    a, b = dp // NB, dp % NB
    x, core = hq * 2 + t // 2, t % 2
    m = hq * NT_DEV + t
    e_here = a * LINE + m

    far = (t + 2) % NT_DEV
    blocks = (far, far + 1 - 2 * (far % 2), t + 1 - 2 * (t % 2), t)

    def load(c):
        start = blocks[c // PIECES] * TOK + c % PIECES * CHUNK
        rows = pl.ds(pl.multiple_of(start, CHUNK), CHUNK)
        return (
            pltpu.make_async_copy(h_ref.at[rows], hv.at[c], load_sem.at[0, c]),
            pltpu.make_async_copy(g_ref.at[rows], gv.at[c], load_sem.at[1, c]),
        )

    loads = [load(c) for c in range(NT_DEV * PIECES)]
    w_in = pltpu.make_async_copy(wi_ref, wiv, w_sem.at[0])
    w_out = pltpu.make_async_copy(wo_ref, wov, w_sem.at[1])
    q_rows = pl.ds(pl.multiple_of(t * QS, QS), QS)
    q_own = pltpu.make_async_copy(q_ref.at[q_rows], qv.at[b], misc_sem.at[0])
    o_own = pltpu.make_async_copy(owner_ref, owner_s, misc_sem.at[1])

    a_at = [(a + i) % NA for i in range(NA)]
    b_at = [(b + i) % NB for i in range(NB)]
    x_at = [(x + i) % NX for i in range(NX)]
    lo_at = [(t // 2 + i) % 2 for i in range(2)]
    core_at = [core, 1 - core]
    plane = [
        (a_at[i], x_at[j] % 2 * 2 + core_at[k], x_at[j] // 2)
        for i, j, k in sorted(
            itertools.product(range(NA), range(NX), range(2)),
            key=lambda v: -(min(v[0], NA - v[0]) + min(v[1], NX - v[1])),
        )
        if (i, j, k) != (0, 0, 0)
    ]
    column = [
        (b_at[i], lo_at[j] * 2 + core_at[k])
        for i, j, k in itertools.product(ring(NB), range(1, -1, -1), range(2))
        if (i, j, k) != (0, 0, 0)
    ]
    beyond = column[: -(NT_DEV - 1)]

    barrier = pltpu.get_barrier_semaphore()

    greeted = [{"tensor": j, "query": k} for i, j, k in plane if i is a_at[0]]
    greeted += [{"dp": dp_of(i, b)} for i in a_at[1:]]
    greeted += [{"dp": dp_of(a, b_at[i])} for i in (2, NB - 2, 1, NB - 1)]

    def greet(some):
        for to in some:
            pl.semaphore_signal(barrier, inc=1, device_id=to, device_id_type=MESH)

    w_in.start()
    loads[0][0].start()
    w_out.start()
    loads[0][1].start()
    for c in range(1, AHEAD):
        greet(greeted[c - 1 :: AHEAD - 1])
        for copy in loads[c]:
            copy.start()
    o_own.start()
    q_own.start()

    def queries_to(step, source, i):
        return pltpu.make_async_remote_copy(
            src_ref=qv.at[source],
            dst_ref=qv.at[source],
            send_sem=q_send,
            recv_sem=q_recv.at[step],
            device_id={"dp": dp_of(a, b_at[i])},
            device_id_type=MESH,
        )

    def queries_to(step, source, i):
        return pltpu.make_async_remote_copy(
            src_ref=qv.at[source],
            dst_ref=qv.at[source],
            send_sem=q_send,
            recv_sem=q_recv.at[step],
            device_id={"dp": dp_of(a, b_at[i])},
            device_id_type=MESH,
        )

    rs = []
    for c in range(NT_DEV * PIECES):
        if c == 0:
            w_in.wait()
        loads[c][0].wait()
        left = lax.dot_general(hv[c], wiv[...], NT, preferred_element_type=F32)
        if c == 0:
            w_out.wait()
        loads[c][1].wait()
        if c + AHEAD < NT_DEV * PIECES:
            for copy in loads[c + AHEAD]:
                copy.start()
        right = lax.dot_general(gv[c], wov[...], NT, preferred_element_type=F32)
        both = jnp.concatenate([left, right], axis=1)
        i, rows = c // PIECES, pl.ds(c % PIECES * CHUNK, CHUNK)
        if i < 2:
            cross[i, rows, :] = both.astype(BF16)
        elif i == 2:
            mate[rows, :] = both
        else:
            own[rows, :] = both
        if c % PIECES < PIECES - 1 or i == 3:
            continue
        if i == 0:
            pl.semaphore_wait(barrier, len(greeted))
        rs.append(
            pltpu.make_async_remote_copy(
                src_ref=cross.at[i] if i < 2 else mate,
                dst_ref=cross_in.at[i] if i < 2 else mate_in,
                send_sem=rs_send.at[i],
                recv_sem=rs_recv.at[i],
                device_id={"tensor": blocks[i]},
                device_id_type=MESH,
            )
        )
        rs[-1].start()
        if i == 0:
            o_own.wait()
            row = lax.broadcasted_iota(jnp.int32, (8, 128), 0)
            tile = jnp.zeros((8, 128), jnp.int32)
            for e in range(8):
                tile = jnp.where(row == e, owner_s[e], tile)
            owner_t[...] = tile
            owner_in[a] = tile
            for to in a_at[1:]:
                pltpu.make_async_remote_copy(
                    src_ref=owner_t,
                    dst_ref=owner_in.at[a],
                    send_sem=ow_send,
                    recv_sem=ow_recv,
                    device_id={"dp": dp_of(to, b)},
                    device_id_type=MESH,
                ).start()
        if i == 0:
            q_own.wait()
            for step, j in enumerate((2, NB - 2, 1, NB - 1)):
                queries_to(step, b, j).start()

    def settle(ref, sem):
        pltpu.make_async_copy(ref, ref, sem).wait()

    for copy in rs:
        copy.wait_recv()
    whole = (
        own[...] + mate_in[...] + cross_in[0].astype(F32) + cross_in[1].astype(F32)
    ).astype(BF16)
    outer[...] = lax.dot_general(whole, whole, TN, preferred_element_type=F32) * (1.0 / TOK)
    lane = lax.broadcasted_iota(jnp.int32, (NB, 128), 1)
    for i in range(NA):
        even = outer[pl.ds(2 * i * NB, NB, stride=2), :]
        odd = outer[pl.ds(2 * i * NB + 1, NB, stride=2), :]
        sketch[i] = jnp.where(lane < RANK, pltpu.roll(even, RANK, 1), odd)
    settle(owner_in.at[pl.ds(0, NA - 1)], ow_recv)
    land[e_here] = sketch[a]

    for i, j, k in plane:
        pltpu.make_async_remote_copy(
            src_ref=sketch.at[i],
            dst_ref=land.at[e_here],
            send_sem=s1_send,
            recv_sem=s1_recv,
            device_id={"dp": dp_of(i, b), "tensor": j, "query": k},
            device_id_type=MESH,
        ).start()

    settle(qv.at[0], q_recv.at[0])
    queries_to(4, b_at[NB - 2], 1).start()
    queries_to(5, b_at[NB - 2], 2).start()
    settle(qv.at[0], q_recv.at[1])
    queries_to(6, b_at[2], NB - 1).start()
    settle(land.at[pl.ds(0, NA * LINE - 1)], s1_recv)
    for step in range(2, NB - 1):
        settle(qv.at[0], q_recv.at[step])

    total = jnp.zeros((NA * LINE, QS), F32)
    for i in range(NB):
        total += lax.dot_general(
            land[:, i, :].astype(BF16), qv[i], NT, preferred_element_type=F32
        )
    part[...] = total.reshape(NA, 8, QS)
    lanes = lax.broadcasted_iota(jnp.int32, (NA * LINE, 128), 1)
    named = dp_of(lanes // NB, lanes % NB)
    onehot = (owner_in[...].reshape(NA * LINE, 128) == named).astype(F32)
    summed = lax.dot_general(
        onehot, total, TN, precision=lax.Precision.HIGHEST, preferred_element_type=F32
    )
    for i in range(NA):
        opart[i] = summed[i * NB : (i + 1) * NB]
    part_in[a] = part[a]
    opart_in[a] = opart[a]

    for i in a_at[2:] + a_at[1:2]:
        for src, dst, k in ((part, part_in, 0), (opart, opart_in, 1)):
            pltpu.make_async_remote_copy(
                src_ref=src.at[i],
                dst_ref=dst.at[a],
                send_sem=s2_send.at[k],
                recv_sem=s2_recv.at[k],
                device_id={"dp": dp_of(i, b)},
                device_id_type=MESH,
            ).start()

    settle(part_in.at[pl.ds(0, NA - 1)], s2_recv.at[0])
    settle(opart_in.at[pl.ds(0, NA - 1)], s2_recv.at[1])
    sc[...] = jnp.sum(part_in[...], axis=0)
    owned = jnp.sum(opart_in[...], axis=0)
    for i in range(NB):
        oo[i] = owned[i : i + 1]

    sc_in[t] = sc[...]
    oo_in[b * NT_DEV + t] = oo[b]

    def send_total(i, j):
        pltpu.make_async_remote_copy(
            src_ref=oo.at[i],
            dst_ref=oo_in.at[b * NT_DEV + t],
            send_sem=s3_send.at[1],
            recv_sem=s3_recv.at[1],
            device_id={"dp": dp_of(a, i), "tensor": j},
            device_id_type=MESH,
        ).start()

    for i, j in beyond:
        send_total(i, j)
    for i, j in column[len(beyond) :]:
        pltpu.make_async_remote_copy(
            src_ref=sc,
            dst_ref=sc_in.at[t],
            send_sem=s3_send.at[0],
            recv_sem=s3_recv.at[0],
            device_id={"tensor": j},
            device_id_type=MESH,
        ).start()
        send_total(i, j)
    settle(sc_in.at[pl.ds(0, NT_DEV - 1)], s3_recv.at[0])
    for i in range(NT_DEV):
        scores_ref[:, i * QS : (i + 1) * QS] = sc_in[i]
    settle(oo_in.at[pl.ds(0, NB * NT_DEV - 1)], s3_recv.at[1])
    for i in range(NT_DEV):
        row = oo_in[i]
        for j in range(1, NB):
            row = row + oo_in[j * NT_DEV + i]
        totals_ref[:, i * QS : (i + 1) * QS] = row

    for copy in rs:
        copy.wait_send()
    settle(qv.at[pl.ds(0, NB - 1)], q_send)
    settle(owner_in.at[pl.ds(0, NA - 1)], ow_send)
    settle(land.at[pl.ds(0, NA * LINE - 1)], s1_send)
    settle(part_in.at[pl.ds(0, NA - 1)], s2_send.at[0])
    settle(opart_in.at[pl.ds(0, NA - 1)], s2_send.at[1])
    settle(sc_in.at[pl.ds(0, NT_DEV - 1)], s3_send.at[0])
    settle(oo_in.at[pl.ds(0, NB * NT_DEV - 1)], s3_send.at[1])


def shards(hidden_acts, out_grads, proj_in, proj_out, queries, owner):
    ff, d = hidden_acts.shape[1], out_grads.shape[1]
    pieces = hidden_acts.shape[0] // CHUNK
    entries = queries.shape[1]
    hbm = pl.BlockSpec(memory_space=pl.ANY)
    vmem = pl.BlockSpec(memory_space=pltpu.VMEM)
    dma = pltpu.SemaphoreType.DMA
    return pl.pallas_call(
        kernel,
        out_shape=(
            jax.ShapeDtypeStruct((8, NT_DEV * QS), F32),
            jax.ShapeDtypeStruct((1, NT_DEV * QS), F32),
        ),
        in_specs=[hbm] * 6,
        out_specs=(vmem, vmem),
        scratch_shapes=[
            pltpu.VMEM((pieces, CHUNK, ff), BF16),
            pltpu.VMEM((pieces, CHUNK, d), BF16),
            pltpu.VMEM((RANK, ff), BF16),
            pltpu.VMEM((RANK, d), BF16),
            pltpu.VMEM((2, TOK, 2 * RANK), BF16),
            pltpu.VMEM((TOK, 2 * RANK), F32),
            pltpu.VMEM((TOK, 2 * RANK), F32),
            pltpu.VMEM((2, TOK, 2 * RANK), BF16),
            pltpu.VMEM((TOK, 2 * RANK), F32),
            pltpu.VMEM((128, 128), F32),
            pltpu.VMEM((NA, NB, 128), F32),
            pltpu.VMEM((NA * LINE, NB, 128), F32),
            pltpu.VMEM((NB, QS, entries), BF16),
            pltpu.SMEM((8,), jnp.int32),
            pltpu.VMEM((8, 128), jnp.int32),
            pltpu.VMEM((NA, 8, 128), jnp.int32),
            pltpu.VMEM((NA, 8, QS), F32),
            pltpu.VMEM((NA, NB, QS), F32),
            pltpu.VMEM((NA, 8, QS), F32),
            pltpu.VMEM((NA, NB, QS), F32),
            pltpu.VMEM((8, QS), F32),
            pltpu.VMEM((NB, 1, QS), F32),
            pltpu.VMEM((NT_DEV, 8, QS), F32),
            pltpu.VMEM((NB * NT_DEV, 1, QS), F32),
            dma((2, pieces)),
            dma((2,)),
            dma((2,)),
            dma((3,)),
            dma((3,)),
            dma,
            dma((NB - 1,)),
            dma,
            dma,
            dma,
            dma,
            dma((2,)),
            dma((2,)),
            dma((2,)),
            dma((2,)),
        ],
        compiler_params=pltpu.CompilerParams(
            collective_id=0, has_side_effects=True, vmem_limit_bytes=55168 << 10
        ),
        name="attribution",
    )(hidden_acts, out_grads, proj_in.T, proj_out.T, queries, owner)


def solution(mesh):
    in_specs = (
        P(("dp", "query"), "tensor"),
        P(("dp", "query"), "tensor"),
        P("tensor", None),
        P("tensor", None),
        P("query", "dp"),
        P("dp"),
    )
    out_specs = (P("dp", "query"), P("dp", "query"))
    return jax.shard_map(shards, mesh=mesh, in_specs=in_specs, out_specs=out_specs, check_vma=False)
```

```python
import itertools

import jax
import jax.numpy as jnp
from jax import lax
from jax.experimental import pallas as pl
from jax.experimental.pallas import tpu as pltpu
from jax.sharding import PartitionSpec as P

MESH = pl.DeviceIdType.MESH
NT = (((1,), (1,)), ((), ()))
TN = (((0,), (0,)), ((), ()))

RANK = 64
TOK = 256
NY, NZ = 4, 8
NT_DEV = 4
LINE = 8
NA, NB = NY, NZ
NX = 4
QS = 256
AHEAD = 2
F32, BF16 = jnp.float32, jnp.bfloat16


def dp_of(a, b):
    return a * NB + b


def ring(n):
    return sorted(range(n), key=lambda i: -min(i, n - i))


def kernel(
    h_ref, g_ref, wi_ref, wo_ref, q_ref, owner_ref,
    scores_ref, totals_ref,
    hv, gv, wiv, wov, cross, mate, own, cross_in, mate_in,
    outer, sketch, land, qv, owner_s, owner_t, owner_in,
    part, opart, part_in, opart_in, sc, oo, sc_in, oo_in,
    load_sem, w_sem, misc_sem, rs_send, rs_recv, q_send, q_recv, ow_send, ow_recv,
    s1_send, s1_recv, s2_send, s2_recv, s3_send, s3_recv,
):
    dp, t, hq = lax.axis_index("dp"), lax.axis_index("tensor"), lax.axis_index("query")
    a, b = dp // NB, dp % NB
    x, core = hq * 2 + t // 2, t % 2
    m = hq * NT_DEV + t
    e_here = a * LINE + m

    far = (t + 2) % NT_DEV
    blocks = (far, far + 1 - 2 * (far % 2), t + 1 - 2 * (t % 2), t)

    def load(c):
        rows = pl.ds(pl.multiple_of(blocks[c] * TOK, TOK), TOK)
        return (
            pltpu.make_async_copy(h_ref.at[rows], hv.at[c], load_sem.at[0, c]),
            pltpu.make_async_copy(g_ref.at[rows], gv.at[c], load_sem.at[1, c]),
        )

    loads = [load(c) for c in range(NT_DEV)]
    w_in = pltpu.make_async_copy(wi_ref, wiv, w_sem.at[0])
    w_out = pltpu.make_async_copy(wo_ref, wov, w_sem.at[1])
    q_rows = pl.ds(pl.multiple_of(t * QS, QS), QS)
    q_own = pltpu.make_async_copy(q_ref.at[q_rows], qv.at[b], misc_sem.at[0])
    o_own = pltpu.make_async_copy(owner_ref, owner_s, misc_sem.at[1])

    a_at = [(a + i) % NA for i in range(NA)]
    b_at = [(b + i) % NB for i in range(NB)]
    x_at = [(x + i) % NX for i in range(NX)]
    lo_at = [(t // 2 + i) % 2 for i in range(2)]
    core_at = [core, 1 - core]
    plane = [
        (a_at[i], x_at[j] % 2 * 2 + core_at[k], x_at[j] // 2)
        for i, j, k in sorted(
            itertools.product(range(NA), range(NX), range(2)),
            key=lambda v: -(min(v[0], NA - v[0]) + min(v[1], NX - v[1])),
        )
        if (i, j, k) != (0, 0, 0)
    ]
    column = [
        (b_at[i], lo_at[j] * 2 + core_at[k])
        for i, j, k in itertools.product(ring(NB), range(1, -1, -1), range(2))
        if (i, j, k) != (0, 0, 0)
    ]
    beyond = column[: -(NT_DEV - 1)]

    barrier = pltpu.get_barrier_semaphore()

    greeted = [{"tensor": j, "query": k} for i, j, k in plane if i is a_at[0]]
    greeted += [{"dp": dp_of(i, b)} for i in a_at[1:]]
    greeted += [{"dp": dp_of(a, b_at[i])} for i in (2, NB - 2, 1, NB - 1)]

    def greet(some):
        for to in some:
            pl.semaphore_signal(barrier, inc=1, device_id=to, device_id_type=MESH)

    w_in.start()
    loads[0][0].start()
    w_out.start()
    loads[0][1].start()
    for c in range(1, AHEAD):
        greet(greeted[c - 1 :: AHEAD - 1])
        for copy in loads[c]:
            copy.start(priority=1)
    o_own.start(priority=1)
    q_own.start(priority=1)

    def queries_to(step, source, i):
        return pltpu.make_async_remote_copy(
            src_ref=qv.at[source],
            dst_ref=qv.at[source],
            send_sem=q_send,
            recv_sem=q_recv.at[step],
            device_id={"dp": dp_of(a, b_at[i])},
            device_id_type=MESH,
        )

    def queries_to(step, source, i):
        return pltpu.make_async_remote_copy(
            src_ref=qv.at[source],
            dst_ref=qv.at[source],
            send_sem=q_send,
            recv_sem=q_recv.at[step],
            device_id={"dp": dp_of(a, b_at[i])},
            device_id_type=MESH,
        )

    rs = [
        pltpu.make_async_remote_copy(
            src_ref=cross.at[i] if i < 2 else mate,
            dst_ref=cross_in.at[i] if i < 2 else mate_in,
            send_sem=rs_send.at[i],
            recv_sem=rs_recv.at[i],
            device_id={"tensor": blocks[i]},
            device_id_type=MESH,
        )
        for i in range(NT_DEV - 1)
    ]

    def meet(ready):
        pl.semaphore_wait(barrier, len(greeted))
        for copy in rs[:ready]:
            copy.start()
        for to in a_at[1:]:
            pltpu.make_async_remote_copy(
                src_ref=owner_t,
                dst_ref=owner_in.at[a],
                send_sem=ow_send,
                recv_sem=ow_recv,
                device_id={"dp": dp_of(to, b)},
                device_id_type=MESH,
            ).start()
        for step, j in enumerate((2, NB - 2, 1, NB - 1)):
            queries_to(step, b, j).start()

    early = b < 1
    for c in range(NT_DEV):
        if c == 0:
            w_in.wait()
            w_out.wait()
        for copy in loads[c]:
            copy.wait()
        if c + AHEAD < NT_DEV:
            for copy in loads[c + AHEAD]:
                copy.start(priority=1)
        left = lax.dot_general(wiv[...], hv[c], NT, preferred_element_type=F32)
        right = lax.dot_general(wov[...], gv[c], NT, preferred_element_type=F32)
        both = jnp.concatenate([left, right], axis=0)
        if c < 2:
            cross[c] = both.astype(BF16)
        elif c == 2:
            mate[...] = both
        else:
            own[...] = both
        if c == 0:
            o_own.wait()
            row = lax.broadcasted_iota(jnp.int32, (8, 128), 0)
            tile = jnp.zeros((8, 128), jnp.int32)
            for e in range(8):
                tile = jnp.where(row == e, owner_s[e], tile)
            owner_t[...] = tile
            owner_in[a] = tile
            q_own.wait()
            pl.when(jnp.logical_not(early))(lambda: meet(1))
        elif c < 3:
            pl.when(jnp.logical_not(early))(rs[c].start)
        else:
            pl.when(early)(lambda: meet(3))

    def settle(ref, sem):
        pltpu.make_async_copy(ref, ref, sem).wait()

    settle(qv.at[0], q_recv.at[0])
    queries_to(5, b_at[NB - 2], 2).start()
    queries_to(4, b_at[NB - 2], 1).start()
    settle(qv.at[0], q_recv.at[1])
    queries_to(6, b_at[2], NB - 1).start()

    for copy in rs:
        copy.wait_recv()
    whole = (
        own[...] + mate_in[...] + cross_in[0].astype(F32) + cross_in[1].astype(F32)
    ).astype(BF16)
    twice = jnp.concatenate([whole[RANK:], whole[RANK:]], axis=0)
    outer[...] = lax.dot_general(
        whole[:RANK], twice, NT, preferred_element_type=F32
    ) * (1.0 / TOK)
    lane = lax.broadcasted_iota(jnp.int32, (NB, 128), 1)
    for i in range(NA):
        even = outer[pl.ds(2 * i * NB, NB, stride=2), :]
        odd = outer[pl.ds(2 * i * NB + 1, NB, stride=2), :]
        sketch[i] = jnp.where(lane < RANK, even, odd)
    settle(owner_in.at[pl.ds(0, NA - 1)], ow_recv)
    land[e_here] = sketch[a]

    for i, j, k in plane:
        pltpu.make_async_remote_copy(
            src_ref=sketch.at[i],
            dst_ref=land.at[e_here],
            send_sem=s1_send,
            recv_sem=s1_recv,
            device_id={"dp": dp_of(i, b), "tensor": j, "query": k},
            device_id_type=MESH,
        ).start()

    lanes = lax.broadcasted_iota(jnp.int32, (NA * LINE, 128), 1)
    named = dp_of(lanes // NB, lanes % NB)
    onehot = (owner_in[...].reshape(NA * LINE, 128) == named).astype(F32).astype(BF16)
    for step in range(2, NB - 1):
        settle(qv.at[0], q_recv.at[step])
    settle(land.at[pl.ds(0, NA * LINE - 1)], s1_recv)

    total = lax.dot_general(
        jnp.concatenate([land[:, i, :] for i in range(NB)], axis=1).astype(BF16),
        jnp.concatenate([qv[i] for i in range(NB)], axis=1),
        NT,
        preferred_element_type=F32,
    )
    part[...] = total.reshape(NA, 8, QS)
    high = total.astype(BF16)
    rest = total - high.astype(F32)
    mid = rest.astype(BF16)
    low = (rest - mid.astype(F32)).astype(BF16)
    summed = lax.dot_general(
        jnp.concatenate([onehot] * 3, axis=0),
        jnp.concatenate([high, mid, low], axis=0),
        TN,
        preferred_element_type=F32,
    )
    for i in range(NA):
        opart[i] = summed[i * NB : (i + 1) * NB]
    for src, dst, k in ((opart, opart_in, 1), (part, part_in, 0)):
        dst[a] = src[a]
        for i in a_at[2:] + a_at[1:2]:
            pltpu.make_async_remote_copy(
                src_ref=src.at[i],
                dst_ref=dst.at[a],
                send_sem=s2_send.at[k],
                recv_sem=s2_recv.at[k],
                device_id={"dp": dp_of(i, b)},
                device_id_type=MESH,
            ).start()

    settle(opart_in.at[pl.ds(0, NA - 1)], s2_recv.at[1])
    owned = jnp.sum(opart_in[...], axis=0)
    for i in range(NB):
        oo[i] = owned[i : i + 1]

    def send_total(i, j):
        pltpu.make_async_remote_copy(
            src_ref=oo.at[i],
            dst_ref=oo_in.at[b * NT_DEV + t],
            send_sem=s3_send.at[1],
            recv_sem=s3_recv.at[1],
            device_id={"dp": dp_of(a, i), "tensor": j},
            device_id_type=MESH,
        ).start()

    for i, j in beyond:
        send_total(i, j)
    settle(part_in.at[pl.ds(0, NA - 1)], s2_recv.at[0])
    sc[...] = jnp.sum(part_in[...], axis=0)
    for i, j in column[len(beyond) :]:
        pltpu.make_async_remote_copy(
            src_ref=sc,
            dst_ref=sc_in.at[t],
            send_sem=s3_send.at[0],
            recv_sem=s3_recv.at[0],
            device_id={"tensor": j},
            device_id_type=MESH,
        ).start()
        send_total(i, j)
    sc_in[t] = sc[...]
    oo_in[b * NT_DEV + t] = oo[b]
    settle(sc_in.at[pl.ds(0, NT_DEV - 1)], s3_recv.at[0])
    for i in range(NT_DEV):
        scores_ref[:, i * QS : (i + 1) * QS] = sc_in[i]
    settle(oo_in.at[pl.ds(0, NB * NT_DEV - 1)], s3_recv.at[1])
    for i in range(NT_DEV):
        row = oo_in[i]
        for j in range(1, NB):
            row = row + oo_in[j * NT_DEV + i]
        totals_ref[:, i * QS : (i + 1) * QS] = row

    for copy in rs:
        copy.wait_send()
    settle(qv.at[pl.ds(0, NB - 1)], q_send)
    settle(owner_in.at[pl.ds(0, NA - 1)], ow_send)
    settle(land.at[pl.ds(0, NA * LINE - 1)], s1_send)
    settle(part_in.at[pl.ds(0, NA - 1)], s2_send.at[0])
    settle(opart_in.at[pl.ds(0, NA - 1)], s2_send.at[1])
    settle(sc_in.at[pl.ds(0, NT_DEV - 1)], s3_send.at[0])
    settle(oo_in.at[pl.ds(0, NB * NT_DEV - 1)], s3_send.at[1])


def shards(hidden_acts, out_grads, proj_in, proj_out, queries, owner):
    ff, d = hidden_acts.shape[1], out_grads.shape[1]
    blocks = hidden_acts.shape[0] // TOK
    entries = queries.shape[1]
    hbm = pl.BlockSpec(memory_space=pl.ANY)
    vmem = pl.BlockSpec(memory_space=pltpu.VMEM)
    dma = pltpu.SemaphoreType.DMA
    return pl.pallas_call(
        kernel,
        out_shape=(
            jax.ShapeDtypeStruct((8, NT_DEV * QS), F32),
            jax.ShapeDtypeStruct((1, NT_DEV * QS), F32),
        ),
        in_specs=[hbm] * 6,
        out_specs=(vmem, vmem),
        scratch_shapes=[
            pltpu.VMEM((blocks, TOK, ff), BF16),
            pltpu.VMEM((blocks, TOK, d), BF16),
            pltpu.VMEM((RANK, ff), BF16),
            pltpu.VMEM((RANK, d), BF16),
            pltpu.VMEM((2, 2 * RANK, TOK), BF16),
            pltpu.VMEM((2 * RANK, TOK), F32),
            pltpu.VMEM((2 * RANK, TOK), F32),
            pltpu.VMEM((2, 2 * RANK, TOK), BF16),
            pltpu.VMEM((2 * RANK, TOK), F32),
            pltpu.VMEM((RANK, 2 * RANK), F32),
            pltpu.VMEM((NA, NB, 128), F32),
            pltpu.VMEM((NA * LINE, NB, 128), F32),
            pltpu.VMEM((NB, QS, entries), BF16),
            pltpu.SMEM((8,), jnp.int32),
            pltpu.VMEM((8, 128), jnp.int32),
            pltpu.VMEM((NA, 8, 128), jnp.int32),
            pltpu.VMEM((NA, 8, QS), F32),
            pltpu.VMEM((NA, NB, QS), F32),
            pltpu.VMEM((NA, 8, QS), F32),
            pltpu.VMEM((NA, NB, QS), F32),
            pltpu.VMEM((8, QS), F32),
            pltpu.VMEM((NB, 1, QS), F32),
            pltpu.VMEM((NT_DEV, 8, QS), F32),
            pltpu.VMEM((NB * NT_DEV, 1, QS), F32),
            dma((2, blocks)),
            dma((2,)),
            dma((2,)),
            dma((3,)),
            dma((3,)),
            dma,
            dma((NB - 1,)),
            dma,
            dma,
            dma,
            dma,
            dma((2,)),
            dma((2,)),
            dma((2,)),
            dma((2,)),
        ],
        compiler_params=pltpu.CompilerParams(
            collective_id=0, has_side_effects=True, vmem_limit_bytes=55168 << 10
        ),
        name="attribution",
    )(hidden_acts, out_grads, proj_in.T, proj_out.T, queries, owner)


def solution(mesh):
    in_specs = (
        P(("dp", "query"), "tensor"),
        P(("dp", "query"), "tensor"),
        P("tensor", None),
        P("tensor", None),
        P("query", "dp"),
        P("dp"),
    )
    out_specs = (P("dp", "query"), P("dp", "query"))
    return jax.shard_map(shards, mesh=mesh, in_specs=in_specs, out_specs=out_specs, check_vma=False)
```

```python
import itertools

import jax
import jax.numpy as jnp
from jax import lax
from jax.experimental import pallas as pl
from jax.experimental.pallas import tpu as pltpu
from jax.sharding import PartitionSpec as P

MESH = pl.DeviceIdType.MESH
NT = (((1,), (1,)), ((), ()))
TN = (((0,), (0,)), ((), ()))

RANK = 64
TOK = 256
NY, NZ = 4, 8
NT_DEV = 4
LINE = 8
NA, NB = NY, NZ
NX = 4
QS = 256
AHEAD = 2
F32, BF16 = jnp.float32, jnp.bfloat16


def dp_of(a, b):
    return a * NB + b


def ring(n):
    return sorted(range(n), key=lambda i: -min(i, n - i))


def kernel(
    h_ref, g_ref, wi_ref, wo_ref, q_ref, owner_ref,
    scores_ref, totals_ref,
    hv, gv, wiv, wov, cross, mate, own, cross_in, mate_in,
    outer, sketch, land, qv, owner_s, owner_t, owner_in,
    part, opart, part_in, opart_in, sc, oo, sc_in, oo_in,
    load_sem, w_sem, misc_sem, rs_send, rs_recv, q_send, q_recv, ow_send, ow_recv,
    s1_send, s1_recv, s2_send, s2_recv, s3_send, s3_recv,
):
    dp, t, hq = lax.axis_index("dp"), lax.axis_index("tensor"), lax.axis_index("query")
    a, b = dp // NB, dp % NB
    x, core = hq * 2 + t // 2, t % 2
    m = hq * NT_DEV + t
    e_here = a * LINE + m

    far = (t + 2) % NT_DEV
    blocks = (far, far + 1 - 2 * (far % 2), t + 1 - 2 * (t % 2), t)

    def load(c):
        rows = pl.ds(pl.multiple_of(blocks[c] * TOK, TOK), TOK)
        return (
            pltpu.make_async_copy(h_ref.at[rows], hv.at[c], load_sem.at[0, c]),
            pltpu.make_async_copy(g_ref.at[rows], gv.at[c], load_sem.at[1, c]),
        )

    loads = [load(c) for c in range(NT_DEV)]
    w_in = pltpu.make_async_copy(wi_ref, wiv, w_sem.at[0])
    w_out = pltpu.make_async_copy(wo_ref, wov, w_sem.at[1])
    q_rows = pl.ds(pl.multiple_of(t * QS, QS), QS)
    q_own = pltpu.make_async_copy(q_ref.at[q_rows], qv.at[b], misc_sem.at[0])
    o_own = pltpu.make_async_copy(owner_ref, owner_s, misc_sem.at[1])

    a_at = [(a + i) % NA for i in range(NA)]
    b_at = [(b + i) % NB for i in range(NB)]
    x_at = [(x + i) % NX for i in range(NX)]
    lo_at = [(t // 2 + i) % 2 for i in range(2)]
    core_at = [core, 1 - core]
    plane = [
        (a_at[i], x_at[j] % 2 * 2 + core_at[k], x_at[j] // 2)
        for i, j, k in sorted(
            itertools.product(range(NA), range(NX), range(2)),
            key=lambda v: -(min(v[0], NA - v[0]) + min(v[1], NX - v[1])),
        )
        if (i, j, k) != (0, 0, 0)
    ]
    column = [
        (b_at[i], lo_at[j] * 2 + core_at[k])
        for i, j, k in itertools.product(ring(NB), range(1, -1, -1), range(2))
        if (i, j, k) != (0, 0, 0)
    ]
    beyond = column[: -(NT_DEV - 1)]

    barrier = pltpu.get_barrier_semaphore()

    greeted = [{"tensor": j, "query": k} for i, j, k in plane if i is a_at[0]]
    greeted += [{"dp": dp_of(i, b)} for i in a_at[1:]]
    greeted += [{"dp": dp_of(a, b_at[i])} for i in (2, NB - 2, 1, NB - 1)]

    def greet(some):
        for to in some:
            pl.semaphore_signal(barrier, inc=1, device_id=to, device_id_type=MESH)

    w_in.start()
    loads[0][0].start()
    w_out.start()
    loads[0][1].start()
    for c in range(1, AHEAD):
        greet(greeted[c - 1 :: AHEAD - 1])
        for copy in loads[c]:
            copy.start(priority=1)
    o_own.start(priority=1)
    q_own.start(priority=1)

    def queries_to(step, source, i):
        return pltpu.make_async_remote_copy(
            src_ref=qv.at[source],
            dst_ref=qv.at[source],
            send_sem=q_send,
            recv_sem=q_recv.at[step],
            device_id={"dp": dp_of(a, b_at[i])},
            device_id_type=MESH,
        )

    def queries_to(step, source, i):
        return pltpu.make_async_remote_copy(
            src_ref=qv.at[source],
            dst_ref=qv.at[source],
            send_sem=q_send,
            recv_sem=q_recv.at[step],
            device_id={"dp": dp_of(a, b_at[i])},
            device_id_type=MESH,
        )

    rs = [
        pltpu.make_async_remote_copy(
            src_ref=cross.at[i] if i < 2 else mate,
            dst_ref=cross_in.at[i] if i < 2 else mate_in,
            send_sem=rs_send.at[i],
            recv_sem=rs_recv.at[i],
            device_id={"tensor": blocks[i]},
            device_id_type=MESH,
        )
        for i in range(NT_DEV - 1)
    ]

    def meet(ready):
        pl.semaphore_wait(barrier, len(greeted))
        for step, j in enumerate((2, NB - 2, 1, NB - 1)):
            queries_to(step, b, j).start()
        for copy in rs[:ready]:
            copy.start()
        for to in a_at[1:]:
            pltpu.make_async_remote_copy(
                src_ref=owner_t,
                dst_ref=owner_in.at[a],
                send_sem=ow_send,
                recv_sem=ow_recv,
                device_id={"dp": dp_of(to, b)},
                device_id_type=MESH,
            ).start()

    early = b < 1
    for c in range(NT_DEV):
        if c == 0:
            o_own.wait()
            row = lax.broadcasted_iota(jnp.int32, (8, 128), 0)
            tile = jnp.zeros((8, 128), jnp.int32)
            for e in range(8):
                tile = jnp.where(row == e, owner_s[e], tile)
            owner_t[...] = tile
            owner_in[a] = tile
            q_own.wait()
            pl.when(jnp.logical_not(early))(lambda: meet(0))
            w_in.wait()
            w_out.wait()
        for copy in loads[c]:
            copy.wait()
        if c + AHEAD < NT_DEV:
            for copy in loads[c + AHEAD]:
                copy.start(priority=1)
        left = lax.dot_general(wiv[...], hv[c], NT, preferred_element_type=F32)
        right = lax.dot_general(wov[...], gv[c], NT, preferred_element_type=F32)
        both = jnp.concatenate([left, right], axis=0)
        if c < 2:
            cross[c] = both.astype(BF16)
        elif c == 2:
            mate[...] = both
        else:
            own[...] = both
        if c == 0:
            pl.when(jnp.logical_not(early))(rs[0].start)
        elif c < 3:
            pl.when(jnp.logical_not(early))(rs[c].start)
        else:
            pl.when(early)(lambda: meet(3))

    def settle(ref, sem):
        pltpu.make_async_copy(ref, ref, sem).wait()

    settle(qv.at[0], q_recv.at[0])
    queries_to(5, b_at[NB - 2], 2).start()
    queries_to(4, b_at[NB - 2], 1).start()
    settle(qv.at[0], q_recv.at[1])
    queries_to(6, b_at[2], NB - 1).start()

    for copy in rs:
        copy.wait_recv()
    whole = (
        own[...] + mate_in[...] + cross_in[0].astype(F32) + cross_in[1].astype(F32)
    ).astype(BF16)
    twice = jnp.concatenate([whole[RANK:], whole[RANK:]], axis=0)
    outer[...] = lax.dot_general(
        whole[:RANK], twice, NT, preferred_element_type=F32
    ) * (1.0 / TOK)
    lane = lax.broadcasted_iota(jnp.int32, (NB, 128), 1)
    for i in range(NA):
        even = outer[pl.ds(2 * i * NB, NB, stride=2), :]
        odd = outer[pl.ds(2 * i * NB + 1, NB, stride=2), :]
        sketch[i] = jnp.where(lane < RANK, even, odd)
    settle(owner_in.at[pl.ds(0, NA - 1)], ow_recv)

    for i, j, k in plane:
        pltpu.make_async_remote_copy(
            src_ref=sketch.at[i],
            dst_ref=land.at[e_here],
            send_sem=s1_send,
            recv_sem=s1_recv,
            device_id={"dp": dp_of(i, b), "tensor": j, "query": k},
            device_id_type=MESH,
        ).start()

    land[e_here] = sketch[a]
    lanes = lax.broadcasted_iota(jnp.int32, (NA * LINE, 128), 1)
    named = dp_of(lanes // NB, lanes % NB)
    onehot = (owner_in[...].reshape(NA * LINE, 128) == named).astype(F32).astype(BF16)
    for step in range(2, NB - 1):
        settle(qv.at[0], q_recv.at[step])
    settle(land.at[pl.ds(0, NA * LINE - 1)], s1_recv)

    total = lax.dot_general(
        jnp.concatenate([land[:, i, :] for i in range(NB)], axis=1).astype(BF16),
        jnp.concatenate([qv[i] for i in range(NB)], axis=1),
        NT,
        preferred_element_type=F32,
    )
    high = total.astype(BF16)
    rest = total - high.astype(F32)
    mid = rest.astype(BF16)
    low = (rest - mid.astype(F32)).astype(BF16)
    summed = lax.dot_general(
        jnp.concatenate([onehot] * 3, axis=0),
        jnp.concatenate([high, mid, low], axis=0),
        TN,
        preferred_element_type=F32,
    )
    for i in range(NA):
        opart[i] = summed[i * NB : (i + 1) * NB]
    for src, dst, k in ((opart, opart_in, 1), (part, part_in, 0)):
        if src is part:
            part[...] = total.reshape(NA, 8, QS)
        for i in a_at[2:] + a_at[1:2]:
            pltpu.make_async_remote_copy(
                src_ref=src.at[i],
                dst_ref=dst.at[a],
                send_sem=s2_send.at[k],
                recv_sem=s2_recv.at[k],
                device_id={"dp": dp_of(i, b)},
                device_id_type=MESH,
            ).start()

    opart_in[a] = opart[a]
    part_in[a] = part[a]

    settle(opart_in.at[pl.ds(0, NA - 1)], s2_recv.at[1])
    owned = jnp.sum(opart_in[...], axis=0)
    for i in range(NB):
        oo[i] = owned[i : i + 1]

    def send_total(i, j):
        pltpu.make_async_remote_copy(
            src_ref=oo.at[i],
            dst_ref=oo_in.at[b * NT_DEV + t],
            send_sem=s3_send.at[1],
            recv_sem=s3_recv.at[1],
            device_id={"dp": dp_of(a, i), "tensor": j},
            device_id_type=MESH,
        ).start()

    for i, j in beyond:
        send_total(i, j)
    settle(part_in.at[pl.ds(0, NA - 1)], s2_recv.at[0])
    sc[...] = jnp.sum(part_in[...], axis=0)
    for i, j in column[len(beyond) :]:
        pltpu.make_async_remote_copy(
            src_ref=sc,
            dst_ref=sc_in.at[t],
            send_sem=s3_send.at[0],
            recv_sem=s3_recv.at[0],
            device_id={"tensor": j},
            device_id_type=MESH,
        ).start()
        send_total(i, j)
    sc_in[t] = sc[...]
    oo_in[b * NT_DEV + t] = oo[b]
    settle(sc_in.at[pl.ds(0, NT_DEV - 1)], s3_recv.at[0])
    for i in range(NT_DEV):
        scores_ref[:, i * QS : (i + 1) * QS] = sc_in[i]
    settle(oo_in.at[pl.ds(0, NB * NT_DEV - 1)], s3_recv.at[1])
    for i in range(NT_DEV):
        row = oo_in[i]
        for j in range(1, NB):
            row = row + oo_in[j * NT_DEV + i]
        totals_ref[:, i * QS : (i + 1) * QS] = row

    for copy in rs:
        copy.wait_send()
    settle(qv.at[pl.ds(0, NB - 1)], q_send)
    settle(owner_in.at[pl.ds(0, NA - 1)], ow_send)
    settle(land.at[pl.ds(0, NA * LINE - 1)], s1_send)
    settle(part_in.at[pl.ds(0, NA - 1)], s2_send.at[0])
    settle(opart_in.at[pl.ds(0, NA - 1)], s2_send.at[1])
    settle(sc_in.at[pl.ds(0, NT_DEV - 1)], s3_send.at[0])
    settle(oo_in.at[pl.ds(0, NB * NT_DEV - 1)], s3_send.at[1])


def shards(hidden_acts, out_grads, proj_in, proj_out, queries, owner):
    ff, d = hidden_acts.shape[1], out_grads.shape[1]
    blocks = hidden_acts.shape[0] // TOK
    entries = queries.shape[1]
    hbm = pl.BlockSpec(memory_space=pl.ANY)
    vmem = pl.BlockSpec(memory_space=pltpu.VMEM)
    dma = pltpu.SemaphoreType.DMA
    return pl.pallas_call(
        kernel,
        out_shape=(
            jax.ShapeDtypeStruct((8, NT_DEV * QS), F32),
            jax.ShapeDtypeStruct((1, NT_DEV * QS), F32),
        ),
        in_specs=[hbm] * 6,
        out_specs=(vmem, vmem),
        scratch_shapes=[
            pltpu.VMEM((blocks, TOK, ff), BF16),
            pltpu.VMEM((blocks, TOK, d), BF16),
            pltpu.VMEM((RANK, ff), BF16),
            pltpu.VMEM((RANK, d), BF16),
            pltpu.VMEM((2, 2 * RANK, TOK), BF16),
            pltpu.VMEM((2 * RANK, TOK), F32),
            pltpu.VMEM((2 * RANK, TOK), F32),
            pltpu.VMEM((2, 2 * RANK, TOK), BF16),
            pltpu.VMEM((2 * RANK, TOK), F32),
            pltpu.VMEM((RANK, 2 * RANK), F32),
            pltpu.VMEM((NA, NB, 128), F32),
            pltpu.VMEM((NA * LINE, NB, 128), F32),
            pltpu.VMEM((NB, QS, entries), BF16),
            pltpu.SMEM((8,), jnp.int32),
            pltpu.VMEM((8, 128), jnp.int32),
            pltpu.VMEM((NA, 8, 128), jnp.int32),
            pltpu.VMEM((NA, 8, QS), F32),
            pltpu.VMEM((NA, NB, QS), F32),
            pltpu.VMEM((NA, 8, QS), F32),
            pltpu.VMEM((NA, NB, QS), F32),
            pltpu.VMEM((8, QS), F32),
            pltpu.VMEM((NB, 1, QS), F32),
            pltpu.VMEM((NT_DEV, 8, QS), F32),
            pltpu.VMEM((NB * NT_DEV, 1, QS), F32),
            dma((2, blocks)),
            dma((2,)),
            dma((2,)),
            dma((3,)),
            dma((3,)),
            dma,
            dma((NB - 1,)),
            dma,
            dma,
            dma,
            dma,
            dma((2,)),
            dma((2,)),
            dma((2,)),
            dma((2,)),
        ],
        compiler_params=pltpu.CompilerParams(
            collective_id=0, has_side_effects=True, vmem_limit_bytes=55168 << 10
        ),
        name="attribution",
    )(hidden_acts, out_grads, proj_in.T, proj_out.T, queries, owner)


def solution(mesh):
    in_specs = (
        P(("dp", "query"), "tensor"),
        P(("dp", "query"), "tensor"),
        P("tensor", None),
        P("tensor", None),
        P("query", "dp"),
        P("dp"),
    )
    out_specs = (P("dp", "query"), P("dp", "query"))
    return jax.shard_map(shards, mesh=mesh, in_specs=in_specs, out_specs=out_specs, check_vma=False)
```
